1024 devices in a mesh: section: 32 (over y, z_lo), fsdp: 32 (over z_hi, x, core).
Axes of the slice: x: 4, y: 4, z: 32 (z_hi: 4, z_lo: 8; z = z_hi * 8 + z_lo), core: 2. Of those that a mesh axis runs over, the one named last changes fastest.
Arguments:
- tokens: bfloat16 [256, 8192], P('section', 'fsdp'), may hold values from -6 to 6
- gate_weight: bfloat16 [8192, 28672], P('fsdp', 'section'), may hold values from -0.0625 to 0.0625
- up_weight: bfloat16 [8192, 28672], P('fsdp', 'section'), may hold values from -0.0625 to 0.0625
- down_weight: bfloat16 [28672, 8192], P('section', 'fsdp'), may hold values from -0.03125 to 0.03125
- out_grad: bfloat16 [256, 8192], P('section', 'fsdp'), may hold values from -6 to 6
Outputs:
- output: bfloat16 [256, 8192], P('section', 'fsdp')
- token_grads: bfloat16 [256, 8192], P('section', 'fsdp')
- gate_grads: bfloat16 [8192, 28672], P('fsdp', 'section')
- up_grads: bfloat16 [8192, 28672], P('fsdp', 'section')
- down_grads: bfloat16 [28672, 8192], P('section', 'fsdp')
The draws below stay inside these ranges and needn't reach their ends.
All inputs are finite; a program needn't handle non-finite values.
Results may differ from the reference program's by a relative error of at most 0.0065.
Values may be sent and summed in bfloat16 or wider, within the bound.
No kernel may reach another device: no remote copies, remote signals or barrier semaphores. Data moves between devices by JAX's collectives and lax.ppermute only.
A program may use at most 32 MiB of HBM per device.

```python
import jax
import jax.numpy as jnp
from jax import lax

D = 8192
FF = 28672
TOKENS = 256


def level_of(key, shape, cuts, least, largest):
    loudness, own = 1.0, jax.random.fold_in(key, 6)
    for position, shards_of in cuts:
        heights = jnp.exp(jax.random.uniform(jax.random.fold_in(own, position), (shards_of,), jnp.float32, least / len(cuts), largest / len(cuts)))
        loudness = loudness * jnp.repeat(heights, shape[position] // shards_of).reshape([-1 if axis == position else 1 for axis in range(len(shape))])
    return loudness


def gaussian(rng, extent, width, most, pieces=(), held_as=jnp.bfloat16):
    factor_of = level_of(rng, extent, pieces, -0.22, 0.18) if pieces else 1.0
    values = jax.random.normal(rng, extent, jnp.float32) * width * factor_of
    return jnp.minimum(jnp.maximum(values, -most), most).astype(held_as)


def setup_inputs(seed: int = 0) -> dict:
    arg_keys = jax.random.split(jax.random.key(seed), 6)
    tokens = gaussian(arg_keys[0], (TOKENS, D), 1.0, 6.0, ((0, 32), (1, 32)))
    gate_weight = gaussian(arg_keys[1], (D, FF), D ** -0.5, 0.0625, ((0, 32), (1, 32)))
    up_weight = gaussian(arg_keys[2], (D, FF), D ** -0.5, 0.0625, ((0, 32), (1, 32)))
    down_weight = gaussian(arg_keys[3], (FF, D), FF ** -0.5, 0.03125, ((0, 32), (1, 32)))
    out_grad = gaussian(arg_keys[4], (TOKENS, D), 1.0, 6.0, ((0, 32), (1, 32)))
    return dict(tokens=tokens, gate_weight=gate_weight, up_weight=up_weight, down_weight=down_weight, out_grad=out_grad)


def contract_last(left, right):
    return lax.dot_general(left, right, (((1,), (1,)), ((), ())), preferred_element_type=jnp.float32)


def contract_first(left, right):
    return lax.dot_general(left, right, (((0,), (0,)), ((), ())), preferred_element_type=jnp.float32)


def reference(tokens, gate_weight, up_weight, down_weight, out_grad):
    gate_sum = jnp.dot(tokens, gate_weight, preferred_element_type=jnp.float32)
    up_sum = jnp.dot(tokens, up_weight, preferred_element_type=jnp.float32)
    gate_sigmoid = jax.nn.sigmoid(gate_sum)
    hidden = (gate_sum * gate_sigmoid * up_sum).astype(jnp.bfloat16)
    output = jnp.dot(hidden, down_weight, preferred_element_type=jnp.float32).astype(jnp.bfloat16)
    hidden_delta = contract_last(out_grad, down_weight)
    gate_delta = (hidden_delta * up_sum * gate_sigmoid * (1.0 + gate_sum * (1.0 - gate_sigmoid))).astype(jnp.bfloat16)
    up_delta = (hidden_delta * gate_sum * gate_sigmoid).astype(jnp.bfloat16)
    token_grads = (contract_last(gate_delta, gate_weight) + contract_last(up_delta, up_weight)).astype(jnp.bfloat16)
    gate_grads = contract_first(tokens, gate_delta).astype(jnp.bfloat16)
    up_grads = contract_first(tokens, up_delta).astype(jnp.bfloat16)
    down_grads = contract_first(hidden, out_grad).astype(jnp.bfloat16)
    return (output, token_grads, gate_grads, up_grads, down_grads)
```

```python
import jax
import jax.numpy as jnp
from jax import lax
from jax.sharding import Mesh, PartitionSpec as P

SECTION = ("y", "zl")
FSDP = ("zh", "x", "core")
BF16 = jnp.bfloat16
F32 = jnp.float32


def contract_last(left, right):
    return lax.dot_general(
        left, right, (((1,), (1,)), ((), ())), preferred_element_type=F32
    )


def contract_first(left, right):
    return lax.dot_general(
        left, right, (((0,), (0,)), ((), ())), preferred_element_type=F32
    )


def swap_core(block):
    return lax.ppermute(block, "core", [(0, 1), (1, 0)])


def sum_over(block, axis):
    ways = lax.axis_size(axis)
    rows, columns = block.shape
    pieces = block.astype(BF16).reshape(ways, rows // ways, columns)
    return lax.all_to_all(pieces, axis, 0, 0).astype(F32).sum(0)


def shards(tokens, gate_weight, up_weight, down_weight, out_grad):
    own, width = tokens.shape
    sections = lax.axis_size(SECTION)
    rows = own * sections
    half = rows // 2
    both = jnp.broadcast_to(
        jnp.stack([tokens, out_grad])[None], (sections, 2, own, width)
    )
    both = lax.all_to_all(both, SECTION, 0, 0)
    both = jnp.swapaxes(both, 0, 1).reshape(2, rows, width)
    shift = lax.axis_index("core") * half
    both = jnp.roll(both, shift, axis=1)
    all_tokens, all_grads = both[0], both[1]
    part = jnp.concatenate(
        [
            jnp.dot(all_tokens, gate_weight, preferred_element_type=F32),
            jnp.dot(all_tokens, up_weight, preferred_element_type=F32),
            contract_last(all_grads, down_weight),
        ],
        axis=1,
    )
    units = gate_weight.shape[1]
    part = part[:half] + swap_core(part[half:].astype(BF16)).astype(F32)
    part = sum_over(part, "x")
    part = sum_over(part, "zh")
    gate_sum, up_sum, hidden_delta = (
        part[:, :units],
        part[:, units : 2 * units],
        part[:, 2 * units :],
    )
    gate_sigmoid = jax.nn.sigmoid(gate_sum)
    hidden = (gate_sum * gate_sigmoid * up_sum).astype(BF16)
    gate_delta = (
        hidden_delta * up_sum * gate_sigmoid * (1.0 + gate_sum * (1.0 - gate_sigmoid))
    ).astype(BF16)
    up_delta = (hidden_delta * gate_sum * gate_sigmoid).astype(BF16)
    whole = jnp.concatenate([hidden, gate_delta, up_delta], axis=1)
    whole = lax.all_gather(whole, "zh", axis=0, tiled=True)
    whole = lax.all_gather(whole, "x", axis=0, tiled=True)
    whole = jnp.concatenate([whole, swap_core(whole)], axis=0)
    hidden, gate_delta, up_delta = (
        whole[:, :units],
        whole[:, units : 2 * units],
        whole[:, 2 * units :],
    )
    forward_part = jnp.dot(hidden, down_weight, preferred_element_type=F32)
    backward_part = contract_last(gate_delta, gate_weight) + contract_last(
        up_delta, up_weight
    )
    ends = jnp.stack([forward_part, backward_part]).astype(BF16)
    ends = jnp.roll(ends, shift, axis=1)
    ends = jnp.swapaxes(ends.reshape(2, sections, own, width), 0, 1)
    ends = lax.all_to_all(ends, SECTION, 0, 0).astype(F32).sum(0).astype(BF16)
    gate_grads = contract_first(all_tokens, gate_delta).astype(BF16)
    up_grads = contract_first(all_tokens, up_delta).astype(BF16)
    down_grads = contract_first(hidden, all_grads).astype(BF16)
    return (ends[0], ends[1], gate_grads, up_grads, down_grads)


def solution(mesh):
    fine = Mesh(
        mesh.devices.reshape(4, 8, 4, 4, 2), ("y", "zl", "zh", "x", "core")
    )
    return jax.shard_map(
        shards,
        mesh=fine,
        in_specs=(
            P(SECTION, FSDP),
            P(FSDP, SECTION),
            P(FSDP, SECTION),
            P(SECTION, FSDP),
            P(SECTION, FSDP),
        ),
        out_specs=(
            P(SECTION, FSDP),
            P(SECTION, FSDP),
            P(FSDP, SECTION),
            P(FSDP, SECTION),
            P(SECTION, FSDP),
        ),
        check_vma=False,
    )
```

```python
import jax
import jax.numpy as jnp
from jax import lax
from jax.sharding import Mesh, PartitionSpec as P

SECTION = ("y", "zl")
FSDP = ("zh", "x", "core")
BF16 = jnp.bfloat16
F32 = jnp.float32


def contract_last(left, right):
    return lax.dot_general(
        left, right, (((1,), (1,)), ((), ())), preferred_element_type=F32
    )


def contract_first(left, right):
    return lax.dot_general(
        left, right, (((0,), (0,)), ((), ())), preferred_element_type=F32
    )


def swap_core(block):
    return lax.ppermute(block, "core", [(0, 1), (1, 0)])


def sum_over(block, axis):
    ways = lax.axis_size(axis)
    rows, columns = block.shape
    pieces = block.reshape(ways, rows // ways, columns)
    me = lax.axis_index(axis)
    mine = lax.dynamic_index_in_dim(pieces, me, 0, keepdims=False)
    others = lax.all_to_all(pieces.astype(BF16), axis, 0, 0).astype(F32)
    foreign = (lax.iota(jnp.int32, ways) != me)[:, None, None]
    return mine + jnp.where(foreign, others, 0.0).sum(0)


def total_over_far(block):
    def swap(part, flip):
        pairs = [(i, i ^ flip) for i in range(4)]
        return lax.ppermute(part.astype(BF16), "zh", pairs).astype(F32)

    half = block.shape[0] // 2
    top, low = block[:half], block[half:]
    top = top + swap(top, 1)
    low = low + swap(low, 3)
    top = top + swap(top, 3)
    low = low + swap(low, 1)
    return jnp.concatenate([top, low], axis=0)


def shards(tokens, gate_weight, up_weight, down_weight, out_grad):
    own, width = tokens.shape
    sections = lax.axis_size(SECTION)
    rows = own * sections
    half = rows // 2
    both = jnp.broadcast_to(
        jnp.stack([tokens, out_grad])[None], (sections, 2, own, width)
    )
    both = lax.all_to_all(both, SECTION, 0, 0)
    both = jnp.swapaxes(both, 0, 1).reshape(2, rows, width)
    shift = lax.axis_index("core") * half
    both = jnp.roll(both, shift, axis=1)
    all_tokens, all_grads = both[0], both[1]
    part = jnp.concatenate(
        [
            jnp.dot(all_tokens, gate_weight, preferred_element_type=F32),
            jnp.dot(all_tokens, up_weight, preferred_element_type=F32),
            contract_last(all_grads, down_weight),
        ],
        axis=1,
    )
    units = gate_weight.shape[1]
    part = part[:half] + swap_core(part[half:])
    part = sum_over(part, "x")
    part = total_over_far(part)
    gate_sum, up_sum, hidden_delta = (
        part[:, :units],
        part[:, units : 2 * units],
        part[:, 2 * units :],
    )
    gate_sigmoid = jax.nn.sigmoid(gate_sum)
    hidden = (gate_sum * gate_sigmoid * up_sum).astype(BF16)
    gate_delta = (
        hidden_delta * up_sum * gate_sigmoid * (1.0 + gate_sum * (1.0 - gate_sigmoid))
    ).astype(BF16)
    up_delta = (hidden_delta * gate_sum * gate_sigmoid).astype(BF16)
    whole = jnp.concatenate([hidden, gate_delta, up_delta], axis=1)
    whole = lax.all_gather(whole, "x", axis=0, tiled=True)
    whole = jnp.concatenate([whole, swap_core(whole)], axis=0)
    hidden, gate_delta, up_delta = (
        whole[:, :units],
        whole[:, units : 2 * units],
        whole[:, 2 * units :],
    )
    forward_part = jnp.dot(hidden, down_weight, preferred_element_type=F32)
    backward_part = contract_last(gate_delta, gate_weight) + contract_last(
        up_delta, up_weight
    )
    ends = jnp.stack([forward_part, backward_part]).astype(BF16)
    ends = jnp.roll(ends, shift, axis=1)
    ends = jnp.swapaxes(ends.reshape(2, sections, own, width), 0, 1)
    ends = lax.all_to_all(ends, SECTION, 0, 0).astype(F32).sum(0).astype(BF16)
    gate_grads = contract_first(all_tokens, gate_delta).astype(BF16)
    up_grads = contract_first(all_tokens, up_delta).astype(BF16)
    down_grads = contract_first(hidden, all_grads).astype(BF16)
    return (ends[0], ends[1], gate_grads, up_grads, down_grads)


def solution(mesh):
    fine = Mesh(
        mesh.devices.reshape(4, 8, 4, 4, 2), ("y", "zl", "zh", "x", "core")
    )
    return jax.shard_map(
        shards,
        mesh=fine,
        in_specs=(
            P(SECTION, FSDP),
            P(FSDP, SECTION),
            P(FSDP, SECTION),
            P(SECTION, FSDP),
            P(SECTION, FSDP),
        ),
        out_specs=(
            P(SECTION, FSDP),
            P(SECTION, FSDP),
            P(FSDP, SECTION),
            P(FSDP, SECTION),
            P(SECTION, FSDP),
        ),
        check_vma=False,
    )
```

```python
import jax
import jax.numpy as jnp
from jax import lax
from jax.sharding import Mesh, PartitionSpec as P

SECTION = ("y", "zl")
FSDP = ("zh", "x", "core")
BF16 = jnp.bfloat16
F32 = jnp.float32


def contract_last(left, right):
    return lax.dot_general(
        left, right, (((1,), (1,)), ((), ())), preferred_element_type=F32
    )


def contract_first(left, right):
    return lax.dot_general(
        left, right, (((0,), (0,)), ((), ())), preferred_element_type=F32
    )


def swap_core(block):
    return lax.ppermute(block, "core", [(0, 1), (1, 0)])


def sum_over_x(block):
    ways = lax.axis_size("x")
    rows, columns = block.shape
    pieces = block.reshape(ways, rows // ways, columns)
    me = lax.axis_index("x")
    mine = lax.dynamic_index_in_dim(pieces, me, 0, keepdims=False)
    others = lax.all_to_all(pieces.astype(BF16), "x", 0, 0).astype(F32)
    foreign = (lax.iota(jnp.int32, ways) != me)[:, None, None]
    return mine + jnp.where(foreign, others, 0.0).sum(0)


def swap_far(part, flips):
    pairs = [
        (2 * z + core, 2 * (z ^ flips[core]) + core)
        for z in range(4)
        for core in range(2)
    ]
    return lax.ppermute(part.astype(BF16), ("zh", "core"), pairs)


def total_over_far(block):
    half = block.shape[0] // 2
    top, low = block[:half], block[half:]
    top_in, low_in = swap_far(top, (1, 3)), swap_far(low, (1, 3))
    top = top + top_in
    low_in, _ = lax.optimization_barrier((low_in, top))
    top_in = swap_far(top, (3, 1))
    low = low + low_in
    low_in = swap_far(low, (3, 1))
    top = top + top_in
    low = low + low_in
    return jnp.concatenate([top, low], axis=0)


def shards(tokens, gate_weight, up_weight, down_weight, out_grad):
    own, width = tokens.shape
    units = gate_weight.shape[1]
    sections = lax.axis_size(SECTION)
    rows = own * sections
    half = rows // 2
    both = jnp.concatenate([tokens, out_grad], axis=1)
    both = jnp.broadcast_to(both[None], (sections, own, 2 * width))
    both = lax.all_to_all(both, SECTION, 0, 0).reshape(rows, 2 * width)

    core = lax.axis_index("core")

    def part_of(which):
        side = lax.dynamic_slice_in_dim(both, which * half, half, 0)
        some_tokens, some_grads = side[:, :width], side[:, width:]
        return jnp.concatenate(
            [
                jnp.dot(some_tokens, gate_weight, preferred_element_type=F32),
                jnp.dot(some_tokens, up_weight, preferred_element_type=F32),
                contract_last(some_grads, down_weight),
            ],
            axis=1,
        )

    received = swap_core(part_of(1 - core))
    part = part_of(core) + received
    part = sum_over_x(part)
    part = total_over_far(part)
    gate_sum, up_sum, hidden_delta = (
        part[:, :units],
        part[:, units : 2 * units],
        part[:, 2 * units :],
    )
    gate_sigmoid = jax.nn.sigmoid(gate_sum)
    hidden = (gate_sum * gate_sigmoid * up_sum).astype(BF16)
    gate_delta = (
        hidden_delta * up_sum * gate_sigmoid * (1.0 + gate_sum * (1.0 - gate_sigmoid))
    ).astype(BF16)
    up_delta = (hidden_delta * gate_sum * gate_sigmoid).astype(BF16)
    mine = jnp.concatenate([hidden, gate_delta, up_delta], axis=1)
    mine = lax.all_gather(mine, "x", axis=0, tiled=True)
    theirs = swap_core(mine)
    first = core == 0
    whole = jnp.concatenate(
        [jnp.where(first, mine, theirs), jnp.where(first, theirs, mine)], axis=0
    )
    hidden, gate_delta, up_delta = (
        whole[:, :units],
        whole[:, units : 2 * units],
        whole[:, 2 * units :],
    )
    forward_part = jnp.dot(hidden, down_weight, preferred_element_type=F32)
    backward_part = contract_last(gate_delta, gate_weight) + contract_last(
        up_delta, up_weight
    )
    ends = jnp.concatenate([forward_part, backward_part], axis=1).astype(BF16)
    ends = ends.reshape(sections, own, 2 * width)
    ends = lax.all_to_all(ends, SECTION, 0, 0)
    ends = lax.optimization_barrier(ends.astype(F32)).sum(0).astype(BF16)
    all_tokens, all_grads = both[:, :width], both[:, width:]
    gate_grads = contract_first(all_tokens, gate_delta).astype(BF16)
    up_grads = contract_first(all_tokens, up_delta).astype(BF16)
    down_grads = contract_first(hidden, all_grads).astype(BF16)
    return (ends[:, :width], ends[:, width:], gate_grads, up_grads, down_grads)


def solution(mesh):
    fine = Mesh(
        mesh.devices.reshape(4, 8, 4, 4, 2), ("y", "zl", "zh", "x", "core")
    )
    return jax.shard_map(
        shards,
        mesh=fine,
        in_specs=(
            P(SECTION, FSDP),
            P(FSDP, SECTION),
            P(FSDP, SECTION),
            P(SECTION, FSDP),
            P(SECTION, FSDP),
        ),
        out_specs=(
            P(SECTION, FSDP),
            P(SECTION, FSDP),
            P(FSDP, SECTION),
            P(FSDP, SECTION),
            P(SECTION, FSDP),
        ),
        check_vma=False,
    )
```

```python
import jax
import jax.numpy as jnp
from jax import lax
from jax.sharding import Mesh, PartitionSpec as P

SECTION = ("y", "zl")
FSDP = ("zh", "x", "core")
BF16 = jnp.bfloat16
F32 = jnp.float32


def contract_last(left, right):
    return lax.dot_general(
        left, right, (((1,), (1,)), ((), ())), preferred_element_type=F32
    )


def contract_first(left, right):
    return lax.dot_general(
        left, right, (((0,), (0,)), ((), ())), preferred_element_type=F32
    )


def swap_core(block):
    return lax.ppermute(block, "core", [(0, 1), (1, 0)])


def sum_over_x(block):
    ways = lax.axis_size("x")
    rows, columns = block.shape
    pieces = block.astype(BF16).reshape(ways, rows // ways, columns)
    return lax.all_to_all(pieces, "x", 0, 0).astype(F32).sum(0)


def swap_far(part, flips):
    pairs = [
        (2 * z + core, 2 * (z ^ flips[core]) + core)
        for z in range(4)
        for core in range(2)
    ]
    return lax.ppermute(part.astype(BF16), ("zh", "core"), pairs)


def deltas_of(part):
    units = part.shape[1] // 3
    gate_sum, up_sum, hidden_delta = (
        part[:, :units],
        part[:, units : 2 * units],
        part[:, 2 * units :],
    )
    gate_sigmoid = jax.nn.sigmoid(gate_sum)
    hidden = gate_sum * gate_sigmoid * up_sum
    gate_delta = (
        hidden_delta * up_sum * gate_sigmoid * (1.0 + gate_sum * (1.0 - gate_sigmoid))
    )
    up_delta = hidden_delta * gate_sum * gate_sigmoid
    return jnp.concatenate([hidden, gate_delta, up_delta], axis=1).astype(BF16)


def gather_over_x(block):
    mine = lax.all_gather(block, "x", axis=0, tiled=False)
    return mine, swap_core(mine)


def shards(tokens, gate_weight, up_weight, down_weight, out_grad):
    own, width = tokens.shape
    units = gate_weight.shape[1]
    sections = lax.axis_size(SECTION)
    rows = own * sections
    half = rows // 2
    both = jnp.concatenate([tokens, out_grad], axis=1)
    both = jnp.broadcast_to(both[None], (sections, own, 2 * width))
    both = lax.all_to_all(both, SECTION, 0, 0).reshape(rows, 2 * width)

    core = lax.axis_index("core")

    def part_of(which):
        side = lax.dynamic_slice_in_dim(both, which * half, half, 0)
        some_tokens, some_grads = side[:, :width], side[:, width:]
        return jnp.concatenate(
            [
                jnp.dot(some_tokens, gate_weight, preferred_element_type=F32),
                jnp.dot(some_tokens, up_weight, preferred_element_type=F32),
                contract_last(some_grads, down_weight),
            ],
            axis=1,
        )

    received = swap_core(part_of(1 - core).astype(BF16))
    part = sum_over_x(part_of(core) + received)

    piece = part.shape[0] // 2
    top, low = part[:piece], part[piece:]
    top_in, low_in = swap_far(top, (1, 3)), swap_far(low, (1, 3))
    top = top + top_in
    low_in, _ = lax.optimization_barrier((low_in, top))
    top_in = swap_far(top, (3, 1))
    low = low + low_in
    low_in = swap_far(low, (3, 1))
    top = deltas_of(top + top_in)
    top_mine, top_theirs = gather_over_x(top)
    low_in, _ = lax.optimization_barrier((low_in, top_theirs))
    low = deltas_of(low + low_in)
    low_mine, low_theirs = gather_over_x(low)
    mine = jnp.concatenate([top_mine, low_mine], axis=1)
    theirs = jnp.concatenate([top_theirs, low_theirs], axis=1)
    first = core == 0
    whole = jnp.stack(
        [jnp.where(first, mine, theirs), jnp.where(first, theirs, mine)]
    ).reshape(rows, 3 * units)
    hidden, gate_delta, up_delta = (
        whole[:, :units],
        whole[:, units : 2 * units],
        whole[:, 2 * units :],
    )
    forward_part = jnp.dot(hidden, down_weight, preferred_element_type=F32)
    backward_part = contract_last(gate_delta, gate_weight) + contract_last(
        up_delta, up_weight
    )
    ends = jnp.concatenate([forward_part, backward_part], axis=1).astype(BF16)
    ends = ends.reshape(sections, own, 2 * width)
    ends = lax.all_to_all(ends, SECTION, 0, 0)
    ends = ends.astype(F32).sum(0).astype(BF16)
    all_tokens, all_grads = both[:, :width], both[:, width:]
    gate_grads = contract_first(all_tokens, gate_delta).astype(BF16)
    up_grads = contract_first(all_tokens, up_delta).astype(BF16)
    down_grads = contract_first(hidden, all_grads).astype(BF16)
    return (ends[:, :width], ends[:, width:], gate_grads, up_grads, down_grads)


def solution(mesh):
    fine = Mesh(
        mesh.devices.reshape(4, 8, 4, 4, 2), ("y", "zl", "zh", "x", "core")
    )
    return jax.shard_map(
        shards,
        mesh=fine,
        in_specs=(
            P(SECTION, FSDP),
            P(FSDP, SECTION),
            P(FSDP, SECTION),
            P(SECTION, FSDP),
            P(SECTION, FSDP),
        ),
        out_specs=(
            P(SECTION, FSDP),
            P(SECTION, FSDP),
            P(FSDP, SECTION),
            P(FSDP, SECTION),
            P(SECTION, FSDP),
        ),
        check_vma=False,
    )
```

```python
import jax
import jax.numpy as jnp
from jax import lax
from jax.experimental import pallas as pl
from jax.experimental.pallas import tpu as pltpu
from jax.sharding import Mesh, PartitionSpec as P

SECTION = ("y", "zl")
FSDP = ("zh", "x", "core")
BF16 = jnp.bfloat16
F32 = jnp.float32


def contract_last(left, right):
    return lax.dot_general(
        left, right, (((1,), (1,)), ((), ())), preferred_element_type=F32
    )


def contract_first(left, right):
    return lax.dot_general(
        left, right, (((0,), (0,)), ((), ())), preferred_element_type=F32
    )


def held(*arrays):
    count = len(arrays)

    def body(*refs):
        sources, targets, done = refs[:count], refs[count:-1], refs[-1]
        copies = [
            pltpu.make_async_copy(source, target, done.at[i])
            for i, (source, target) in enumerate(zip(sources, targets))
        ]
        for copy in copies:
            copy.start()
        for copy in copies:
            copy.wait()

    return pl.pallas_call(
        body,
        out_shape=[pltpu.VMEM(a.shape, a.dtype) for a in arrays],
        in_specs=[pl.BlockSpec(memory_space=pl.ANY)] * count,
        out_specs=[pl.BlockSpec(memory_space=pltpu.VMEM)] * count,
        scratch_shapes=[pltpu.SemaphoreType.DMA((count,))],
    )(*arrays)


def swap_core(block):
    return lax.ppermute(block, "core", [(0, 1), (1, 0)])


def sum_over_x(block):
    ways = lax.axis_size("x")
    rows, columns = block.shape
    pieces = block.astype(BF16).reshape(ways, rows // ways, columns)
    return lax.all_to_all(pieces, "x", 0, 0).astype(F32).sum(0)


def swap_far(part, flips):
    pairs = [
        (2 * z + core, 2 * (z ^ flips[core]) + core)
        for z in range(4)
        for core in range(2)
    ]
    return lax.ppermute(part.astype(BF16), ("zh", "core"), pairs)


def deltas_of(part):
    units = part.shape[1] // 3
    gate_sum, up_sum, hidden_delta = (
        part[:, :units],
        part[:, units : 2 * units],
        part[:, 2 * units :],
    )
    gate_sigmoid = jax.nn.sigmoid(gate_sum)
    hidden = gate_sum * gate_sigmoid * up_sum
    gate_delta = (
        hidden_delta * up_sum * gate_sigmoid * (1.0 + gate_sum * (1.0 - gate_sigmoid))
    )
    up_delta = hidden_delta * gate_sum * gate_sigmoid
    return jnp.concatenate([hidden, gate_delta, up_delta], axis=1).astype(BF16)


def copies_over_x(block):
    copies = jnp.broadcast_to(block[None], (lax.axis_size("x"),) + block.shape)
    return lax.all_to_all(copies, "x", 0, 0)


def shards(tokens, gate_weight, up_weight, down_weight, out_grad):
    own, width = tokens.shape
    units = gate_weight.shape[1]
    sections = lax.axis_size(SECTION)
    rows = own * sections
    half = rows // 2
    gate_weight, up_weight, down_weight = held(gate_weight, up_weight, down_weight)
    copies = (sections, own, width)
    both = jnp.concatenate(
        [jnp.broadcast_to(tokens, copies), jnp.broadcast_to(out_grad, copies)], axis=2
    )
    both = lax.all_to_all(both, SECTION, 0, 0).reshape(rows, 2 * width)

    core = lax.axis_index("core")

    def part_of(which):
        side = lax.dynamic_slice_in_dim(both, which * half, half, 0)
        some_tokens, some_grads = side[:, :width], side[:, width:]
        return jnp.concatenate(
            [
                jnp.dot(some_tokens, gate_weight, preferred_element_type=F32),
                jnp.dot(some_tokens, up_weight, preferred_element_type=F32),
                contract_last(some_grads, down_weight),
            ],
            axis=1,
        )

    received = swap_core(part_of(1 - core).astype(BF16))
    part = sum_over_x(part_of(core) + received)

    piece = part.shape[0] // 2
    top, low = part[:piece], part[piece:]
    top_in, low_in = swap_far(top, (1, 3)), swap_far(low, (1, 3))
    top = top + top_in
    low_in, _ = lax.optimization_barrier((low_in, top))
    top_in = swap_far(top, (3, 1))
    low = low + low_in
    low_in = swap_far(low, (3, 1))
    top = deltas_of(top + top_in)
    top_mine = lax.all_gather(top, "x", axis=0, tiled=False)
    top_theirs = swap_core(top_mine)
    low_in, _ = lax.optimization_barrier((low_in, top_mine))
    low = deltas_of(low + low_in)
    low, _ = lax.optimization_barrier((low, top_theirs))
    low_mine = copies_over_x(low)
    low_theirs = swap_core(low_mine)
    mine = jnp.concatenate([top_mine, low_mine], axis=1)
    theirs = jnp.concatenate([top_theirs, low_theirs], axis=1)
    first = core == 0
    whole = jnp.stack(
        [jnp.where(first, mine, theirs), jnp.where(first, theirs, mine)]
    ).reshape(rows, 3 * units)
    hidden, gate_delta, up_delta = (
        whole[:, :units],
        whole[:, units : 2 * units],
        whole[:, 2 * units :],
    )
    forward_part = jnp.dot(hidden, down_weight, preferred_element_type=F32)
    backward_part = contract_last(gate_delta, gate_weight) + contract_last(
        up_delta, up_weight
    )
    ends = jnp.concatenate([forward_part, backward_part], axis=1).astype(BF16)
    ends = ends.reshape(sections, own, 2 * width)
    ends = lax.all_to_all(ends, SECTION, 0, 0)
    ends = ends.astype(F32).sum(0).astype(BF16)
    all_tokens, all_grads = both[:, :width], both[:, width:]
    gate_grads = contract_first(all_tokens, gate_delta).astype(BF16)
    up_grads = contract_first(all_tokens, up_delta).astype(BF16)
    down_grads = contract_first(hidden, all_grads).astype(BF16)
    return (ends[:, :width], ends[:, width:], gate_grads, up_grads, down_grads)


def solution(mesh):
    fine = Mesh(
        mesh.devices.reshape(4, 8, 4, 4, 2), ("y", "zl", "zh", "x", "core")
    )
    return jax.shard_map(
        shards,
        mesh=fine,
        in_specs=(
            P(SECTION, FSDP),
            P(FSDP, SECTION),
            P(FSDP, SECTION),
            P(SECTION, FSDP),
            P(SECTION, FSDP),
        ),
        out_specs=(
            P(SECTION, FSDP),
            P(SECTION, FSDP),
            P(FSDP, SECTION),
            P(FSDP, SECTION),
            P(SECTION, FSDP),
        ),
        check_vma=False,
    )
```

```python
import jax
import jax.numpy as jnp
from jax import lax
from jax.experimental import pallas as pl
from jax.experimental.pallas import tpu as pltpu
from jax.sharding import Mesh, PartitionSpec as P

SECTION = ("y", "zl")
FSDP = ("zh", "x", "core")
BF16 = jnp.bfloat16
F32 = jnp.float32


def contract_last(left, right):
    return lax.dot_general(
        left, right, (((1,), (1,)), ((), ())), preferred_element_type=F32
    )


def contract_first(left, right):
    return lax.dot_general(
        left, right, (((0,), (0,)), ((), ())), preferred_element_type=F32
    )


def held(*arrays):
    count = len(arrays)

    def body(*refs):
        sources, targets, done = refs[:count], refs[count:-1], refs[-1]
        copies = [
            pltpu.make_async_copy(source, target, done.at[i])
            for i, (source, target) in enumerate(zip(sources, targets))
        ]
        for copy in copies:
            copy.start()
        for copy in copies:
            copy.wait()

    return pl.pallas_call(
        body,
        out_shape=[pltpu.VMEM(a.shape, a.dtype) for a in arrays],
        in_specs=[pl.BlockSpec(memory_space=pl.ANY)] * count,
        out_specs=[pl.BlockSpec(memory_space=pltpu.VMEM)] * count,
        scratch_shapes=[pltpu.SemaphoreType.DMA((count,))],
    )(*arrays)


def side_by_side(left, right, count):
    rows, width = left.shape

    def body(left_ref, right_ref, out_ref):
        pair = jnp.concatenate([left_ref[...], right_ref[...]], axis=1)
        out_ref[...] = jnp.broadcast_to(pair[None], (count, rows, 2 * width))

    return pl.pallas_call(
        body,
        out_shape=pltpu.VMEM((count, rows, 2 * width), left.dtype),
        in_specs=[pl.BlockSpec(memory_space=pltpu.VMEM)] * 2,
        out_specs=pl.BlockSpec(memory_space=pltpu.VMEM),
    )(left, right)


def swap_core(block):
    return lax.ppermute(block, "core", [(0, 1), (1, 0)])


def sum_over_x(block):
    ways = lax.axis_size("x")
    rows, columns = block.shape
    pieces = block.astype(BF16).reshape(ways, rows // ways, columns)
    return lax.all_to_all(pieces, "x", 0, 0).astype(F32).sum(0)


def swap_far(part, flips):
    pairs = [
        (2 * z + core, 2 * (z ^ flips[core]) + core)
        for z in range(4)
        for core in range(2)
    ]
    return lax.ppermute(part.astype(BF16), ("zh", "core"), pairs)


def deltas_of(part):
    units = part.shape[1] // 3
    gate_sum, up_sum, hidden_delta = (
        part[:, :units],
        part[:, units : 2 * units],
        part[:, 2 * units :],
    )
    gate_sigmoid = jax.nn.sigmoid(gate_sum)
    hidden = gate_sum * gate_sigmoid * up_sum
    gate_delta = (
        hidden_delta * up_sum * gate_sigmoid * (1.0 + gate_sum * (1.0 - gate_sigmoid))
    )
    up_delta = hidden_delta * gate_sum * gate_sigmoid
    return jnp.concatenate([hidden, gate_delta, up_delta], axis=1).astype(BF16)


def copies_over_x(block):
    copies = jnp.broadcast_to(block[None], (lax.axis_size("x"),) + block.shape)
    return lax.all_to_all(copies, "x", 0, 0)


def shards(tokens, gate_weight, up_weight, down_weight, out_grad):
    own, width = tokens.shape
    units = gate_weight.shape[1]
    sections = lax.axis_size(SECTION)
    rows = own * sections
    half = rows // 2
    gate_weight, up_weight, down_weight = held(gate_weight, up_weight, down_weight)
    both = side_by_side(tokens, out_grad, sections)
    both = lax.all_to_all(both, SECTION, 0, 0).reshape(rows, 2 * width)

    core = lax.axis_index("core")

    def part_of(which):
        side = lax.dynamic_slice_in_dim(both, which * half, half, 0)
        some_tokens, some_grads = side[:, :width], side[:, width:]
        return jnp.concatenate(
            [
                jnp.dot(some_tokens, gate_weight, preferred_element_type=F32),
                jnp.dot(some_tokens, up_weight, preferred_element_type=F32),
                contract_last(some_grads, down_weight),
            ],
            axis=1,
        )

    received = swap_core(part_of(1 - core).astype(BF16))
    part = sum_over_x(part_of(core) + received)

    piece = part.shape[0] // 2
    top, low = part[:piece], part[piece:]
    top_in, low_in = swap_far(top, (1, 3)), swap_far(low, (1, 3))
    top = top + top_in
    low_in, _ = lax.optimization_barrier((low_in, top))
    top_in = swap_far(top, (3, 1))
    low = low + low_in
    low_in = swap_far(low, (3, 1))
    mine = copies_over_x(deltas_of(jnp.concatenate([top + top_in, low + low_in])))
    theirs = swap_core(mine)
    first = core == 0
    whole = jnp.stack(
        [jnp.where(first, mine, theirs), jnp.where(first, theirs, mine)]
    ).reshape(rows, 3 * units)
    hidden, gate_delta, up_delta = (
        whole[:, :units],
        whole[:, units : 2 * units],
        whole[:, 2 * units :],
    )
    forward_part = jnp.dot(hidden, down_weight, preferred_element_type=F32)
    backward_part = contract_last(gate_delta, gate_weight) + contract_last(
        up_delta, up_weight
    )
    ends = jnp.concatenate([forward_part, backward_part], axis=1).astype(BF16)
    ends = ends.reshape(sections, own, 2 * width)
    ends = lax.all_to_all(ends, SECTION, 0, 0)
    ends = ends.astype(F32).sum(0).astype(BF16)
    all_tokens, all_grads = both[:, :width], both[:, width:]
    gate_grads = contract_first(all_tokens, gate_delta).astype(BF16)
    up_grads = contract_first(all_tokens, up_delta).astype(BF16)
    down_grads = contract_first(hidden, all_grads).astype(BF16)
    return (ends[:, :width], ends[:, width:], gate_grads, up_grads, down_grads)


def solution(mesh):
    fine = Mesh(
        mesh.devices.reshape(4, 8, 4, 4, 2), ("y", "zl", "zh", "x", "core")
    )
    return jax.shard_map(
        shards,
        mesh=fine,
        in_specs=(
            P(SECTION, FSDP),
            P(FSDP, SECTION),
            P(FSDP, SECTION),
            P(SECTION, FSDP),
            P(SECTION, FSDP),
        ),
        out_specs=(
            P(SECTION, FSDP),
            P(SECTION, FSDP),
            P(FSDP, SECTION),
            P(FSDP, SECTION),
            P(SECTION, FSDP),
        ),
        check_vma=False,
    )
```

```python
import jax
import jax.numpy as jnp
from jax import lax
from jax.experimental import pallas as pl
from jax.experimental.pallas import tpu as pltpu
from jax.sharding import Mesh, PartitionSpec as P

SECTION = ("y", "zl")
FSDP = ("zh", "x", "core")
BF16 = jnp.bfloat16
F32 = jnp.float32


def contract_last(left, right):
    return lax.dot_general(
        left, right, (((1,), (1,)), ((), ())), preferred_element_type=F32
    )


def contract_first(left, right):
    return lax.dot_general(
        left, right, (((0,), (0,)), ((), ())), preferred_element_type=F32
    )


def held(*arrays):
    count = len(arrays)

    def body(*refs):
        sources, targets, done = refs[:count], refs[count:-1], refs[-1]
        copies = [
            pltpu.make_async_copy(source, target, done.at[i])
            for i, (source, target) in enumerate(zip(sources, targets))
        ]
        for copy in copies:
            copy.start()
        for copy in copies:
            copy.wait()

    return pl.pallas_call(
        body,
        out_shape=[pltpu.VMEM(a.shape, a.dtype) for a in arrays],
        in_specs=[pl.BlockSpec(memory_space=pl.ANY)] * count,
        out_specs=[pl.BlockSpec(memory_space=pltpu.VMEM)] * count,
        scratch_shapes=[pltpu.SemaphoreType.DMA((count,))],
    )(*arrays)


def side_by_side(left, right, count):
    rows, width = left.shape

    def body(left_ref, right_ref, out_ref):
        pair = jnp.concatenate([left_ref[...], right_ref[...]], axis=1)
        out_ref[...] = jnp.broadcast_to(pair[None], (count, rows, 2 * width))

    return pl.pallas_call(
        body,
        out_shape=pltpu.VMEM((count, rows, 2 * width), left.dtype),
        in_specs=[pl.BlockSpec(memory_space=pltpu.VMEM)] * 2,
        out_specs=pl.BlockSpec(memory_space=pltpu.VMEM),
    )(left, right)


def swap_core(block):
    return lax.ppermute(block, "core", [(0, 1), (1, 0)])


def sum_over_x(block):
    ways = lax.axis_size("x")
    rows, columns = block.shape
    pieces = block.astype(BF16).reshape(ways, rows // ways, columns)
    return lax.all_to_all(pieces, "x", 0, 0).astype(F32).sum(0)


def swap_far(part, flips):
    pairs = [
        (2 * z + core, 2 * (z ^ flips[core]) + core)
        for z in range(4)
        for core in range(2)
    ]
    return lax.ppermute(part.astype(BF16), ("zh", "core"), pairs)


def deltas_of(part):
    units = part.shape[1] // 3
    gate_sum, up_sum, hidden_delta = (
        part[:, :units],
        part[:, units : 2 * units],
        part[:, 2 * units :],
    )
    gate_sigmoid = jax.nn.sigmoid(gate_sum)
    hidden = gate_sum * gate_sigmoid * up_sum
    gate_delta = (
        hidden_delta * up_sum * gate_sigmoid * (1.0 + gate_sum * (1.0 - gate_sigmoid))
    )
    up_delta = hidden_delta * gate_sum * gate_sigmoid
    return jnp.concatenate([hidden, gate_delta, up_delta], axis=1).astype(BF16)


def copies_over_x(block):
    copies = jnp.broadcast_to(block[None], (lax.axis_size("x"),) + block.shape)
    return lax.all_to_all(copies, "x", 0, 0)


def shards(tokens, gate_weight, up_weight, down_weight, out_grad):
    own, width = tokens.shape
    units = gate_weight.shape[1]
    sections = lax.axis_size(SECTION)
    rows = own * sections
    half = rows // 2
    gate_weight, up_weight, down_weight = held(gate_weight, up_weight, down_weight)
    runs, lines = lax.axis_size("zl"), lax.axis_size("y")
    both = side_by_side(tokens, out_grad, runs)
    both = lax.all_to_all(both, "zl", 0, 0)
    both = jnp.broadcast_to(both[None], (lines,) + both.shape)
    both = lax.all_to_all(both, "y", 0, 0).reshape(rows, 2 * width)

    core = lax.axis_index("core")

    def part_of(which):
        side = lax.dynamic_slice_in_dim(both, which * half, half, 0)
        some_tokens, some_grads = side[:, :width], side[:, width:]
        return jnp.concatenate(
            [
                jnp.dot(some_tokens, gate_weight, preferred_element_type=F32),
                jnp.dot(some_tokens, up_weight, preferred_element_type=F32),
                contract_last(some_grads, down_weight),
            ],
            axis=1,
        )

    received = swap_core(part_of(1 - core).astype(BF16))
    part = sum_over_x(part_of(core) + received)

    piece = part.shape[0] // 2
    top, low = part[:piece], part[piece:]
    top_in, low_in = swap_far(top, (1, 3)), swap_far(low, (1, 3))
    top = top + top_in
    low_in, _ = lax.optimization_barrier((low_in, top))
    top_in = swap_far(top, (3, 1))
    low = low + low_in
    low_in = swap_far(low, (3, 1))
    mine = copies_over_x(deltas_of(jnp.concatenate([top + top_in, low + low_in])))
    theirs = swap_core(mine)
    first = core == 0
    whole = jnp.stack(
        [jnp.where(first, mine, theirs), jnp.where(first, theirs, mine)]
    ).reshape(rows, 3 * units)
    hidden, gate_delta, up_delta = (
        whole[:, :units],
        whole[:, units : 2 * units],
        whole[:, 2 * units :],
    )
    forward_part = jnp.dot(hidden, down_weight, preferred_element_type=F32)
    backward_part = contract_last(gate_delta, gate_weight) + contract_last(
        up_delta, up_weight
    )
    ends = jnp.concatenate([forward_part, backward_part], axis=1).astype(BF16)
    ends = ends.reshape(lines, runs, own, 2 * width)
    ends = lax.all_to_all(ends, "y", 0, 0).astype(F32).sum(0).astype(BF16)
    ends = lax.all_to_all(ends, "zl", 0, 0).astype(F32).sum(0).astype(BF16)
    all_tokens, all_grads = both[:, :width], both[:, width:]
    gate_grads = contract_first(all_tokens, gate_delta).astype(BF16)
    up_grads = contract_first(all_tokens, up_delta).astype(BF16)
    down_grads = contract_first(hidden, all_grads).astype(BF16)
    return (ends[:, :width], ends[:, width:], gate_grads, up_grads, down_grads)


def solution(mesh):
    fine = Mesh(
        mesh.devices.reshape(4, 8, 4, 4, 2), ("y", "zl", "zh", "x", "core")
    )
    return jax.shard_map(
        shards,
        mesh=fine,
        in_specs=(
            P(SECTION, FSDP),
            P(FSDP, SECTION),
            P(FSDP, SECTION),
            P(SECTION, FSDP),
            P(SECTION, FSDP),
        ),
        out_specs=(
            P(SECTION, FSDP),
            P(SECTION, FSDP),
            P(FSDP, SECTION),
            P(FSDP, SECTION),
            P(SECTION, FSDP),
        ),
        check_vma=False,
    )
```

```python
import jax
import jax.numpy as jnp
from jax import lax
from jax.experimental import pallas as pl
from jax.experimental.pallas import tpu as pltpu
from jax.sharding import Mesh, PartitionSpec as P

SECTION = ("y", "zl")
FSDP = ("zh", "x", "core")
BF16 = jnp.bfloat16
F32 = jnp.float32


def contract_last(left, right):
    return lax.dot_general(
        left, right, (((1,), (1,)), ((), ())), preferred_element_type=F32
    )


def contract_first(left, right):
    return lax.dot_general(
        left, right, (((0,), (0,)), ((), ())), preferred_element_type=F32
    )


def held(*arrays):
    count = len(arrays)

    def body(*refs):
        sources, targets, done = refs[:count], refs[count:-1], refs[-1]
        copies = [
            pltpu.make_async_copy(source, target, done.at[i])
            for i, (source, target) in enumerate(zip(sources, targets))
        ]
        for copy in copies:
            copy.start()
        for copy in copies:
            copy.wait()

    return pl.pallas_call(
        body,
        out_shape=[pltpu.VMEM(a.shape, a.dtype) for a in arrays],
        in_specs=[pl.BlockSpec(memory_space=pl.ANY)] * count,
        out_specs=[pl.BlockSpec(memory_space=pltpu.VMEM)] * count,
        scratch_shapes=[pltpu.SemaphoreType.DMA((count,))],
    )(*arrays)


def side_by_side(left, right, count):
    rows, width = left.shape

    def body(left_ref, right_ref, out_ref):
        pair = jnp.concatenate([left_ref[...], right_ref[...]], axis=1)
        out_ref[...] = jnp.broadcast_to(pair[None], (count, rows, 2 * width))

    return pl.pallas_call(
        body,
        out_shape=pltpu.VMEM((count, rows, 2 * width), left.dtype),
        in_specs=[pl.BlockSpec(memory_space=pltpu.VMEM)] * 2,
        out_specs=pl.BlockSpec(memory_space=pltpu.VMEM),
    )(left, right)


def swap_core(block):
    return lax.ppermute(block, "core", [(0, 1), (1, 0)])


def sum_over_x(block):
    ways = lax.axis_size("x")
    rows, columns = block.shape
    pieces = block.astype(BF16).reshape(ways, rows // ways, columns)
    return lax.all_to_all(pieces, "x", 0, 0).astype(F32).sum(0)


def swap_far(part, flips):
    pairs = [
        (2 * z + core, 2 * (z ^ flips[core]) + core)
        for z in range(4)
        for core in range(2)
    ]
    return lax.ppermute(part.astype(BF16), ("zh", "core"), pairs)


def deltas_of(part):
    units = part.shape[1] // 3
    gate_sum, up_sum, hidden_delta = (
        part[:, :units],
        part[:, units : 2 * units],
        part[:, 2 * units :],
    )
    gate_sigmoid = jax.nn.sigmoid(gate_sum)
    hidden = gate_sum * gate_sigmoid * up_sum
    gate_delta = (
        hidden_delta * up_sum * gate_sigmoid * (1.0 + gate_sum * (1.0 - gate_sigmoid))
    )
    up_delta = hidden_delta * gate_sum * gate_sigmoid
    return jnp.concatenate([hidden, gate_delta, up_delta], axis=1).astype(BF16)


def copies_over_x(block):
    copies = jnp.broadcast_to(block[None], (lax.axis_size("x"),) + block.shape)
    return lax.all_to_all(copies, "x", 0, 0)


def shards(tokens, gate_weight, up_weight, down_weight, out_grad):
    own, width = tokens.shape
    units = gate_weight.shape[1]
    sections = lax.axis_size(SECTION)
    rows = own * sections
    half = rows // 2
    gate_weight, up_weight, down_weight = held(gate_weight, up_weight, down_weight)
    runs, lines = lax.axis_size("zl"), lax.axis_size("y")
    both = side_by_side(tokens, out_grad, runs)
    both = lax.all_to_all(both, "zl", 0, 0)
    both = jnp.broadcast_to(both[None], (lines,) + both.shape)
    both = lax.all_to_all(both, "y", 0, 0).reshape(rows, 2 * width)

    core = lax.axis_index("core")

    def part_of(which):
        side = lax.dynamic_slice_in_dim(both, which * half, half, 0)
        some_tokens, some_grads = side[:, :width], side[:, width:]
        return jnp.concatenate(
            [
                jnp.dot(some_tokens, gate_weight, preferred_element_type=F32),
                jnp.dot(some_tokens, up_weight, preferred_element_type=F32),
                contract_last(some_grads, down_weight),
            ],
            axis=1,
        )

    received = swap_core(part_of(1 - core).astype(BF16))
    part = sum_over_x(part_of(core) + received)

    piece = part.shape[0] // 2
    top, low = part[:piece], part[piece:]
    top_in, low_in = swap_far(top, (1, 3)), swap_far(low, (1, 3))
    top = top + top_in
    low_in, _ = lax.optimization_barrier((low_in, top))
    top_in = swap_far(top, (3, 1))
    low = low + low_in
    low_in = swap_far(low, (3, 1))
    mine = copies_over_x(deltas_of(jnp.concatenate([top + top_in, low + low_in])))
    theirs = swap_core(mine)
    first = core == 0
    whole = jnp.stack(
        [jnp.where(first, mine, theirs), jnp.where(first, theirs, mine)]
    ).reshape(rows, 3 * units)
    hidden, gate_delta, up_delta = (
        whole[:, :units],
        whole[:, units : 2 * units],
        whole[:, 2 * units :],
    )
    forward_part = jnp.dot(hidden, down_weight, preferred_element_type=F32)
    backward_part = contract_last(gate_delta, gate_weight) + contract_last(
        up_delta, up_weight
    )
    ends = jnp.concatenate([forward_part, backward_part], axis=1).astype(BF16)
    ends = ends.reshape(sections, own, 2 * width)
    ends = lax.all_to_all(ends, SECTION, 0, 0).astype(F32).sum(0).astype(BF16)
    all_tokens, all_grads = both[:, :width], both[:, width:]
    gate_grads = contract_first(all_tokens, gate_delta).astype(BF16)
    up_grads = contract_first(all_tokens, up_delta).astype(BF16)
    down_grads = contract_first(hidden, all_grads).astype(BF16)
    return (ends[:, :width], ends[:, width:], gate_grads, up_grads, down_grads)


def solution(mesh):
    fine = Mesh(
        mesh.devices.reshape(4, 8, 4, 4, 2), ("y", "zl", "zh", "x", "core")
    )
    return jax.shard_map(
        shards,
        mesh=fine,
        in_specs=(
            P(SECTION, FSDP),
            P(FSDP, SECTION),
            P(FSDP, SECTION),
            P(SECTION, FSDP),
            P(SECTION, FSDP),
        ),
        out_specs=(
            P(SECTION, FSDP),
            P(SECTION, FSDP),
            P(FSDP, SECTION),
            P(FSDP, SECTION),
            P(SECTION, FSDP),
        ),
        check_vma=False,
    )
```

```python
import jax
import jax.numpy as jnp
from jax import lax
from jax.experimental import pallas as pl
from jax.experimental.pallas import tpu as pltpu
from jax.sharding import Mesh, PartitionSpec as P

SECTION = ("y", "zl")
FSDP = ("zh", "x", "core")
BF16 = jnp.bfloat16
F32 = jnp.float32


def contract_last(left, right):
    return lax.dot_general(
        left, right, (((1,), (1,)), ((), ())), preferred_element_type=F32
    )


def contract_first(left, right):
    return lax.dot_general(
        left, right, (((0,), (0,)), ((), ())), preferred_element_type=F32
    )


def held(*arrays):
    count = len(arrays)

    def body(*refs):
        sources, targets, done = refs[:count], refs[count:-1], refs[-1]
        copies = [
            pltpu.make_async_copy(source, target, done.at[i])
            for i, (source, target) in enumerate(zip(sources, targets))
        ]
        for copy in copies:
            copy.start()
        for copy in copies:
            copy.wait()

    return pl.pallas_call(
        body,
        out_shape=[pltpu.VMEM(a.shape, a.dtype) for a in arrays],
        in_specs=[pl.BlockSpec(memory_space=pl.ANY)] * count,
        out_specs=[pl.BlockSpec(memory_space=pltpu.VMEM)] * count,
        scratch_shapes=[pltpu.SemaphoreType.DMA((count,))],
    )(*arrays)


def side_by_side(left, right, count):
    rows, width = left.shape

    def body(left_ref, right_ref, out_ref):
        pair = jnp.concatenate([left_ref[...], right_ref[...]], axis=1)
        out_ref[...] = jnp.broadcast_to(pair[None], (count, rows, 2 * width))

    return pl.pallas_call(
        body,
        out_shape=pltpu.VMEM((count, rows, 2 * width), left.dtype),
        in_specs=[pl.BlockSpec(memory_space=pltpu.VMEM)] * 2,
        out_specs=pl.BlockSpec(memory_space=pltpu.VMEM),
    )(left, right)


def swap_core(block):
    return lax.ppermute(block, "core", [(0, 1), (1, 0)])


def sum_over_x(block):
    ways = lax.axis_size("x")
    rows, columns = block.shape
    pieces = block.astype(BF16).reshape(ways, rows // ways, columns)
    return lax.all_to_all(pieces, "x", 0, 0).astype(F32).sum(0)


def swap_far(part, flips):
    pairs = [
        (2 * z + core, 2 * (z ^ flips[core]) + core)
        for z in range(4)
        for core in range(2)
    ]
    return lax.ppermute(part.astype(BF16), ("zh", "core"), pairs)


def deltas_of(part):
    units = part.shape[1] // 3
    gate_sum, up_sum, hidden_delta = (
        part[:, :units],
        part[:, units : 2 * units],
        part[:, 2 * units :],
    )
    gate_sigmoid = jax.nn.sigmoid(gate_sum)
    hidden = gate_sum * gate_sigmoid * up_sum
    gate_delta = (
        hidden_delta * up_sum * gate_sigmoid * (1.0 + gate_sum * (1.0 - gate_sigmoid))
    )
    up_delta = hidden_delta * gate_sum * gate_sigmoid
    return jnp.concatenate([hidden, gate_delta, up_delta], axis=1).astype(BF16)


def copies_over_x(block):
    copies = jnp.broadcast_to(block[None], (lax.axis_size("x"),) + block.shape)
    return lax.all_to_all(copies, "x", 0, 0)


def shards(tokens, gate_weight, up_weight, down_weight, out_grad):
    own, width = tokens.shape
    units = gate_weight.shape[1]
    sections = lax.axis_size(SECTION)
    rows = own * sections
    half = rows // 2
    gate_weight, up_weight, down_weight = held(gate_weight, up_weight, down_weight)
    runs, lines = lax.axis_size("zl"), lax.axis_size("y")
    both = side_by_side(tokens, out_grad, runs)
    both = lax.all_to_all(both, "zl", 0, 0)
    both = jnp.broadcast_to(both[None], (lines,) + both.shape)
    both = lax.all_to_all(both, "y", 0, 0).reshape(rows, 2 * width)

    core = lax.axis_index("core")

    def part_of(which):
        side = lax.dynamic_slice_in_dim(both, which * half, half, 0)
        some_tokens, some_grads = side[:, :width], side[:, width:]
        return jnp.concatenate(
            [
                jnp.dot(some_tokens, gate_weight, preferred_element_type=F32),
                jnp.dot(some_tokens, up_weight, preferred_element_type=F32),
                contract_last(some_grads, down_weight),
            ],
            axis=1,
        )

    received = swap_core(part_of(1 - core).astype(BF16))
    part = sum_over_x(part_of(core) + received)

    piece = part.shape[0] // 2
    top, low = part[:piece], part[piece:]
    top_in, low_in = swap_far(top, (1, 3)), swap_far(low, (3, 1))
    top = top + top_in
    low_in, _ = lax.optimization_barrier((low_in, top))
    top_in = swap_far(top, (3, 1))
    low = low + low_in
    low_in = swap_far(low, (1, 3))
    mine = copies_over_x(deltas_of(jnp.concatenate([top + top_in, low + low_in])))
    theirs = swap_core(mine)
    first = core == 0
    whole = jnp.stack(
        [jnp.where(first, mine, theirs), jnp.where(first, theirs, mine)]
    ).reshape(rows, 3 * units)
    hidden, gate_delta, up_delta = (
        whole[:, :units],
        whole[:, units : 2 * units],
        whole[:, 2 * units :],
    )
    forward_part = jnp.dot(hidden, down_weight, preferred_element_type=F32)
    backward_part = contract_last(gate_delta, gate_weight) + contract_last(
        up_delta, up_weight
    )
    ends = jnp.concatenate([forward_part, backward_part], axis=1).astype(BF16)
    ends = ends.reshape(sections, own, 2 * width)
    ends = lax.all_to_all(ends, SECTION, 0, 0).astype(F32).sum(0).astype(BF16)
    all_tokens, all_grads = both[:, :width], both[:, width:]
    gate_grads = contract_first(all_tokens, gate_delta).astype(BF16)
    up_grads = contract_first(all_tokens, up_delta).astype(BF16)
    down_grads = contract_first(hidden, all_grads).astype(BF16)
    return (ends[:, :width], ends[:, width:], gate_grads, up_grads, down_grads)


def solution(mesh):
    fine = Mesh(
        mesh.devices.reshape(4, 8, 4, 4, 2), ("y", "zl", "zh", "x", "core")
    )
    return jax.shard_map(
        shards,
        mesh=fine,
        in_specs=(
            P(SECTION, FSDP),
            P(FSDP, SECTION),
            P(FSDP, SECTION),
            P(SECTION, FSDP),
            P(SECTION, FSDP),
        ),
        out_specs=(
            P(SECTION, FSDP),
            P(SECTION, FSDP),
            P(FSDP, SECTION),
            P(FSDP, SECTION),
            P(SECTION, FSDP),
        ),
        check_vma=False,
    )
```

```python
import jax
import jax.numpy as jnp
from jax import lax
from jax.experimental import pallas as pl
from jax.experimental.pallas import tpu as pltpu
from jax.sharding import Mesh, PartitionSpec as P

SECTION = ("y", "zl")
FSDP = ("zh", "x", "core")
BF16 = jnp.bfloat16
F32 = jnp.float32


def contract_last(left, right):
    return lax.dot_general(
        left, right, (((1,), (1,)), ((), ())), preferred_element_type=F32
    )


def contract_first(left, right):
    return lax.dot_general(
        left, right, (((0,), (0,)), ((), ())), preferred_element_type=F32
    )


def held(*arrays):
    count = len(arrays)

    def body(*refs):
        sources, targets, done = refs[:count], refs[count:-1], refs[-1]
        copies = [
            pltpu.make_async_copy(source, target, done.at[i])
            for i, (source, target) in enumerate(zip(sources, targets))
        ]
        for copy in copies:
            copy.start()
        for copy in copies:
            copy.wait()

    return pl.pallas_call(
        body,
        out_shape=[pltpu.VMEM(a.shape, a.dtype) for a in arrays],
        in_specs=[pl.BlockSpec(memory_space=pl.ANY)] * count,
        out_specs=[pl.BlockSpec(memory_space=pltpu.VMEM)] * count,
        scratch_shapes=[pltpu.SemaphoreType.DMA((count,))],
    )(*arrays)


def side_by_side(left, right, count):
    rows, width = left.shape

    def body(left_ref, right_ref, out_ref):
        pair = jnp.concatenate([left_ref[...], right_ref[...]], axis=1)
        out_ref[...] = jnp.broadcast_to(pair[None], (count, rows, 2 * width))

    return pl.pallas_call(
        body,
        out_shape=pltpu.VMEM((count, rows, 2 * width), left.dtype),
        in_specs=[pl.BlockSpec(memory_space=pltpu.VMEM)] * 2,
        out_specs=pl.BlockSpec(memory_space=pltpu.VMEM),
    )(left, right)


def swap_core(block):
    return lax.ppermute(block, "core", [(0, 1), (1, 0)])


def sum_over_x(block):
    ways = lax.axis_size("x")
    rows, columns = block.shape
    pieces = block.astype(BF16).reshape(ways, rows // ways, columns)
    return lax.all_to_all(pieces, "x", 0, 0).astype(F32).sum(0)


def swap_far(part, flips):
    pairs = [
        (2 * z + core, 2 * (z ^ flips[core]) + core)
        for z in range(4)
        for core in range(2)
    ]
    return lax.ppermute(part.astype(BF16), ("zh", "core"), pairs)


def deltas_of(part):
    units = part.shape[1] // 3
    gate_sum, up_sum, hidden_delta = (
        part[:, :units],
        part[:, units : 2 * units],
        part[:, 2 * units :],
    )
    gate_sigmoid = jax.nn.sigmoid(gate_sum)
    hidden = gate_sum * gate_sigmoid * up_sum
    gate_delta = (
        hidden_delta * up_sum * gate_sigmoid * (1.0 + gate_sum * (1.0 - gate_sigmoid))
    )
    up_delta = hidden_delta * gate_sum * gate_sigmoid
    return jnp.concatenate([hidden, gate_delta, up_delta], axis=1).astype(BF16)


def copies_over_x(block):
    copies = jnp.broadcast_to(block[None], (lax.axis_size("x"),) + block.shape)
    return lax.all_to_all(copies, "x", 0, 0)


def shards(tokens, gate_weight, up_weight, down_weight, out_grad):
    own, width = tokens.shape
    units = gate_weight.shape[1]
    sections = lax.axis_size(SECTION)
    rows = own * sections
    half = rows // 2
    gate_weight, up_weight, down_weight = held(gate_weight, up_weight, down_weight)
    runs, lines = lax.axis_size("zl"), lax.axis_size("y")
    both = side_by_side(tokens, out_grad, runs)
    both = lax.all_to_all(both, "zl", 0, 0)
    both = jnp.broadcast_to(both[None], (lines,) + both.shape)
    both = lax.all_to_all(both, "y", 0, 0).reshape(rows, 2 * width)

    core = lax.axis_index("core")

    def part_of(which):
        side = lax.dynamic_slice_in_dim(both, which * half, half, 0)
        some_tokens, some_grads = side[:, :width], side[:, width:]
        return jnp.concatenate(
            [
                jnp.dot(some_tokens, gate_weight, preferred_element_type=F32),
                jnp.dot(some_tokens, up_weight, preferred_element_type=F32),
                contract_last(some_grads, down_weight),
            ],
            axis=1,
        )

    received = swap_core(part_of(1 - core).astype(BF16))
    part = sum_over_x(part_of(core) + received)

    piece = part.shape[0] // 2
    top, low = part[:piece], part[piece:]
    top_in, low_in = swap_far(top, (1, 3)), swap_far(low, (3, 1))
    top = top + top_in
    low_in, _ = lax.optimization_barrier((low_in, top))
    top_in = swap_far(top, (3, 1))
    low = low + low_in
    low_in = swap_far(low, (1, 3))
    mine = copies_over_x(deltas_of(jnp.concatenate([top + top_in, low + low_in])))
    mine = mine.reshape(half, 3 * units)
    theirs = swap_core(mine)

    def ends_of(some):
        forward_part = jnp.dot(
            some[:, :units], down_weight, preferred_element_type=F32
        )
        backward_part = contract_last(
            some[:, units : 2 * units], gate_weight
        ) + contract_last(some[:, 2 * units :], up_weight)
        return jnp.concatenate([forward_part, backward_part], axis=1).astype(BF16)

    def in_order(own_rows, other_rows):
        first = core == 0
        return jnp.stack(
            [
                jnp.where(first, own_rows, other_rows),
                jnp.where(first, other_rows, own_rows),
            ]
        )

    ends = in_order(ends_of(mine), ends_of(theirs))
    whole = in_order(mine, theirs).reshape(rows, 3 * units)
    hidden, gate_delta, up_delta = (
        whole[:, :units],
        whole[:, units : 2 * units],
        whole[:, 2 * units :],
    )
    ends = ends.reshape(sections, own, 2 * width)
    ends = lax.all_to_all(ends, SECTION, 0, 0).astype(F32).sum(0).astype(BF16)
    all_tokens, all_grads = both[:, :width], both[:, width:]
    gate_grads = contract_first(all_tokens, gate_delta).astype(BF16)
    up_grads = contract_first(all_tokens, up_delta).astype(BF16)
    down_grads = contract_first(hidden, all_grads).astype(BF16)
    return (ends[:, :width], ends[:, width:], gate_grads, up_grads, down_grads)


def solution(mesh):
    fine = Mesh(
        mesh.devices.reshape(4, 8, 4, 4, 2), ("y", "zl", "zh", "x", "core")
    )
    return jax.shard_map(
        shards,
        mesh=fine,
        in_specs=(
            P(SECTION, FSDP),
            P(FSDP, SECTION),
            P(FSDP, SECTION),
            P(SECTION, FSDP),
            P(SECTION, FSDP),
        ),
        out_specs=(
            P(SECTION, FSDP),
            P(SECTION, FSDP),
            P(FSDP, SECTION),
            P(FSDP, SECTION),
            P(SECTION, FSDP),
        ),
        check_vma=False,
    )
```

```python
import jax
import jax.numpy as jnp
from jax import lax
from jax.experimental import pallas as pl
from jax.experimental.pallas import tpu as pltpu
from jax.sharding import Mesh, PartitionSpec as P

SECTION = ("y", "zl")
FSDP = ("zh", "x", "core")
BF16 = jnp.bfloat16
F32 = jnp.float32


def contract_last(left, right):
    return lax.dot_general(
        left, right, (((1,), (1,)), ((), ())), preferred_element_type=F32
    )


def contract_first(left, right):
    return lax.dot_general(
        left, right, (((0,), (0,)), ((), ())), preferred_element_type=F32
    )


def held(*arrays):
    count = len(arrays)

    def body(*refs):
        sources, targets, done = refs[:count], refs[count:-1], refs[-1]
        copies = [
            pltpu.make_async_copy(source, target, done.at[i])
            for i, (source, target) in enumerate(zip(sources, targets))
        ]
        for copy in copies:
            copy.start()
        for copy in copies:
            copy.wait()

    return pl.pallas_call(
        body,
        out_shape=[pltpu.VMEM(a.shape, a.dtype) for a in arrays],
        in_specs=[pl.BlockSpec(memory_space=pl.ANY)] * count,
        out_specs=[pl.BlockSpec(memory_space=pltpu.VMEM)] * count,
        scratch_shapes=[pltpu.SemaphoreType.DMA((count,))],
    )(*arrays)


def side_by_side(left, right, count):
    rows, width = left.shape

    def body(left_ref, right_ref, out_ref):
        pair = jnp.concatenate([left_ref[...], right_ref[...]], axis=1)
        out_ref[...] = jnp.broadcast_to(pair[None], (count, rows, 2 * width))

    return pl.pallas_call(
        body,
        out_shape=pltpu.VMEM((count, rows, 2 * width), left.dtype),
        in_specs=[pl.BlockSpec(memory_space=pltpu.VMEM)] * 2,
        out_specs=pl.BlockSpec(memory_space=pltpu.VMEM),
    )(left, right)


def swap_core(block):
    return lax.ppermute(block, "core", [(0, 1), (1, 0)])


def sum_over_x(block):
    ways = lax.axis_size("x")
    rows, columns = block.shape
    pieces = block.astype(BF16).reshape(ways, rows // ways, columns)
    return lax.all_to_all(pieces, "x", 0, 0).astype(F32).sum(0)


def swap_far(part, flips):
    pairs = [
        (2 * z + core, 2 * (z ^ flips[core]) + core)
        for z in range(4)
        for core in range(2)
    ]
    return lax.ppermute(part.astype(BF16), ("zh", "core"), pairs)


def deltas_of(part):
    units = part.shape[1] // 3
    gate_sum, up_sum, hidden_delta = (
        part[:, :units],
        part[:, units : 2 * units],
        part[:, 2 * units :],
    )
    gate_sigmoid = jax.nn.sigmoid(gate_sum)
    hidden = gate_sum * gate_sigmoid * up_sum
    gate_delta = (
        hidden_delta * up_sum * gate_sigmoid * (1.0 + gate_sum * (1.0 - gate_sigmoid))
    )
    up_delta = hidden_delta * gate_sum * gate_sigmoid
    return jnp.concatenate([hidden, gate_delta, up_delta], axis=1).astype(BF16)


def copies_over_x(block):
    copies = jnp.broadcast_to(block[None], (lax.axis_size("x"),) + block.shape)
    return lax.all_to_all(copies, "x", 0, 0)


def shards(tokens, gate_weight, up_weight, down_weight, out_grad):
    own, width = tokens.shape
    units = gate_weight.shape[1]
    sections = lax.axis_size(SECTION)
    rows = own * sections
    half = rows // 2
    gate_weight, up_weight, down_weight = held(gate_weight, up_weight, down_weight)
    runs, lines = lax.axis_size("zl"), lax.axis_size("y")
    both = side_by_side(tokens, out_grad, runs)
    both = lax.all_to_all(both, "zl", 0, 0)
    both = jnp.broadcast_to(both[None], (lines,) + both.shape)
    both = lax.all_to_all(both, "y", 0, 0).reshape(rows, 2 * width)

    core = lax.axis_index("core")

    def part_of(which):
        side = lax.dynamic_slice_in_dim(both, which * half, half, 0)
        some_tokens, some_grads = side[:, :width], side[:, width:]
        return jnp.concatenate(
            [
                jnp.dot(some_tokens, gate_weight, preferred_element_type=F32),
                jnp.dot(some_tokens, up_weight, preferred_element_type=F32),
                contract_last(some_grads, down_weight),
            ],
            axis=1,
        )

    received = swap_core(part_of(1 - core).astype(BF16))
    part = sum_over_x(part_of(core) + received)

    piece = part.shape[0] // 2
    top, low = part[:piece], part[piece:]
    top_in, low_in = swap_far(top, (1, 3)), swap_far(low, (3, 1))
    top = top + top_in
    sent = top.astype(BF16)
    low_in, _ = lax.optimization_barrier((low_in, sent))
    top_in = swap_far(sent, (3, 1))
    low = low + low_in
    low_in = swap_far(low, (1, 3))
    mine = copies_over_x(deltas_of(jnp.concatenate([top + top_in, low + low_in])))
    mine = mine.reshape(half, 3 * units)
    theirs = swap_core(mine)

    def ends_of(some):
        forward_part = jnp.dot(
            some[:, :units], down_weight, preferred_element_type=F32
        )
        backward_part = contract_last(
            some[:, units : 2 * units], gate_weight
        ) + contract_last(some[:, 2 * units :], up_weight)
        return jnp.concatenate([forward_part, backward_part], axis=1).astype(BF16)

    def in_order(own_rows, other_rows):
        first = core == 0
        return jnp.stack(
            [
                jnp.where(first, own_rows, other_rows),
                jnp.where(first, other_rows, own_rows),
            ]
        )

    ends = in_order(ends_of(mine), ends_of(theirs))
    whole = in_order(mine, theirs).reshape(rows, 3 * units)
    hidden, gate_delta, up_delta = (
        whole[:, :units],
        whole[:, units : 2 * units],
        whole[:, 2 * units :],
    )
    ends = ends.reshape(sections, own, 2 * width)
    ends = lax.all_to_all(ends, SECTION, 0, 0).astype(F32).sum(0).astype(BF16)
    all_tokens, all_grads = both[:, :width], both[:, width:]
    gate_grads = contract_first(all_tokens, gate_delta).astype(BF16)
    up_grads = contract_first(all_tokens, up_delta).astype(BF16)
    down_grads = contract_first(hidden, all_grads).astype(BF16)
    return (ends[:, :width], ends[:, width:], gate_grads, up_grads, down_grads)


def solution(mesh):
    fine = Mesh(
        mesh.devices.reshape(4, 8, 4, 4, 2), ("y", "zl", "zh", "x", "core")
    )
    return jax.shard_map(
        shards,
        mesh=fine,
        in_specs=(
            P(SECTION, FSDP),
            P(FSDP, SECTION),
            P(FSDP, SECTION),
            P(SECTION, FSDP),
            P(SECTION, FSDP),
        ),
        out_specs=(
            P(SECTION, FSDP),
            P(SECTION, FSDP),
            P(FSDP, SECTION),
            P(FSDP, SECTION),
            P(SECTION, FSDP),
        ),
        check_vma=False,
    )
```

```python
import jax
import jax.numpy as jnp
from jax import lax
from jax.experimental import pallas as pl
from jax.experimental.pallas import tpu as pltpu
from jax.sharding import Mesh, PartitionSpec as P

SECTION = ("y", "zl")
FSDP = ("zh", "x", "core")
BF16 = jnp.bfloat16
F32 = jnp.float32


def contract_last(left, right):
    return lax.dot_general(
        left, right, (((1,), (1,)), ((), ())), preferred_element_type=F32
    )


def contract_first(left, right):
    return lax.dot_general(
        left, right, (((0,), (0,)), ((), ())), preferred_element_type=F32
    )


def held(*arrays):
    count = len(arrays)

    def body(*refs):
        sources, targets, done = refs[:count], refs[count:-1], refs[-1]
        copies = [
            pltpu.make_async_copy(source, target, done.at[i])
            for i, (source, target) in enumerate(zip(sources, targets))
        ]
        for copy in copies:
            copy.start()
        for copy in copies:
            copy.wait()

    return pl.pallas_call(
        body,
        out_shape=[pltpu.VMEM(a.shape, a.dtype) for a in arrays],
        in_specs=[pl.BlockSpec(memory_space=pl.ANY)] * count,
        out_specs=[pl.BlockSpec(memory_space=pltpu.VMEM)] * count,
        scratch_shapes=[pltpu.SemaphoreType.DMA((count,))],
    )(*arrays)


def side_by_side(left, right, count):
    rows, width = left.shape

    def body(left_ref, right_ref, out_ref):
        pair = jnp.concatenate([left_ref[...], right_ref[...]], axis=1)
        out_ref[...] = jnp.broadcast_to(pair[None], (count, rows, 2 * width))

    return pl.pallas_call(
        body,
        out_shape=pltpu.VMEM((count, rows, 2 * width), left.dtype),
        in_specs=[pl.BlockSpec(memory_space=pltpu.VMEM)] * 2,
        out_specs=pl.BlockSpec(memory_space=pltpu.VMEM),
    )(left, right)


def swap_core(block):
    return lax.ppermute(block, "core", [(0, 1), (1, 0)])


def sum_over_x(block):
    ways = lax.axis_size("x")
    rows, columns = block.shape
    pieces = block.astype(BF16).reshape(ways, rows // ways, columns)
    return lax.all_to_all(pieces, "x", 0, 0).astype(F32).sum(0)


def swap_far(part, flips):
    pairs = [
        (2 * z + core, 2 * (z ^ flips[core]) + core)
        for z in range(4)
        for core in range(2)
    ]
    return lax.ppermute(part.astype(BF16), ("zh", "core"), pairs)


def deltas_of(part):
    units = part.shape[1] // 3
    gate_sum, up_sum, hidden_delta = (
        part[:, :units],
        part[:, units : 2 * units],
        part[:, 2 * units :],
    )
    gate_sigmoid = jax.nn.sigmoid(gate_sum)
    hidden = gate_sum * gate_sigmoid * up_sum
    gate_delta = (
        hidden_delta * up_sum * gate_sigmoid * (1.0 + gate_sum * (1.0 - gate_sigmoid))
    )
    up_delta = hidden_delta * gate_sum * gate_sigmoid
    return jnp.concatenate([hidden, gate_delta, up_delta], axis=1).astype(BF16)


def copies_over_x(block):
    copies = jnp.broadcast_to(block[None], (lax.axis_size("x"),) + block.shape)
    return lax.all_to_all(copies, "x", 0, 0)


def shards(tokens, gate_weight, up_weight, down_weight, out_grad):
    own, width = tokens.shape
    units = gate_weight.shape[1]
    sections = lax.axis_size(SECTION)
    rows = own * sections
    half = rows // 2
    gate_weight, up_weight, down_weight = held(gate_weight, up_weight, down_weight)
    both = side_by_side(tokens, out_grad, sections)
    both = lax.all_to_all(both, SECTION, 0, 0).reshape(rows, 2 * width)

    core = lax.axis_index("core")

    def part_of(which):
        side = lax.dynamic_slice_in_dim(both, which * half, half, 0)
        some_tokens, some_grads = side[:, :width], side[:, width:]
        return jnp.concatenate(
            [
                jnp.dot(some_tokens, gate_weight, preferred_element_type=F32),
                jnp.dot(some_tokens, up_weight, preferred_element_type=F32),
                contract_last(some_grads, down_weight),
            ],
            axis=1,
        )

    received = swap_core(part_of(1 - core).astype(BF16))
    part = sum_over_x(part_of(core) + received)

    piece = part.shape[0] // 2
    top, low = part[:piece], part[piece:]
    top_in, low_in = swap_far(top, (1, 3)), swap_far(low, (3, 1))
    top = top + top_in
    sent = top.astype(BF16)
    low_in, _ = lax.optimization_barrier((low_in, sent))
    top_in = swap_far(sent, (3, 1))
    low = low + low_in
    low_in = swap_far(low, (1, 3))
    mine = copies_over_x(deltas_of(jnp.concatenate([top + top_in, low + low_in])))
    mine = mine.reshape(half, 3 * units)
    theirs = swap_core(mine)

    def ends_of(some):
        forward_part = jnp.dot(
            some[:, :units], down_weight, preferred_element_type=F32
        )
        backward_part = contract_last(
            some[:, units : 2 * units], gate_weight
        ) + contract_last(some[:, 2 * units :], up_weight)
        return jnp.concatenate([forward_part, backward_part], axis=1).astype(BF16)

    def in_order(own_rows, other_rows):
        first = core == 0
        return jnp.stack(
            [
                jnp.where(first, own_rows, other_rows),
                jnp.where(first, other_rows, own_rows),
            ]
        )

    ends = in_order(ends_of(mine), ends_of(theirs))
    whole = in_order(mine, theirs).reshape(rows, 3 * units)
    hidden, gate_delta, up_delta = (
        whole[:, :units],
        whole[:, units : 2 * units],
        whole[:, 2 * units :],
    )
    ends = ends.reshape(sections, own, 2 * width)
    ends = lax.all_to_all(ends, SECTION, 0, 0).astype(F32).sum(0).astype(BF16)
    all_tokens, all_grads = both[:, :width], both[:, width:]
    gate_grads = contract_first(all_tokens, gate_delta).astype(BF16)
    up_grads = contract_first(all_tokens, up_delta).astype(BF16)
    down_grads = contract_first(hidden, all_grads).astype(BF16)
    return (ends[:, :width], ends[:, width:], gate_grads, up_grads, down_grads)


def solution(mesh):
    fine = Mesh(
        mesh.devices.reshape(4, 8, 4, 4, 2), ("y", "zl", "zh", "x", "core")
    )
    return jax.shard_map(
        shards,
        mesh=fine,
        in_specs=(
            P(SECTION, FSDP),
            P(FSDP, SECTION),
            P(FSDP, SECTION),
            P(SECTION, FSDP),
            P(SECTION, FSDP),
        ),
        out_specs=(
            P(SECTION, FSDP),
            P(SECTION, FSDP),
            P(FSDP, SECTION),
            P(FSDP, SECTION),
            P(SECTION, FSDP),
        ),
        check_vma=False,
    )
```

```python
import jax
import jax.numpy as jnp
from jax import lax
from jax.experimental import pallas as pl
from jax.experimental.pallas import tpu as pltpu
from jax.sharding import Mesh, PartitionSpec as P

SECTION = ("y", "zl")
FSDP = ("zh", "x", "core")
BF16 = jnp.bfloat16
F32 = jnp.float32


def contract_last(left, right):
    return lax.dot_general(
        left, right, (((1,), (1,)), ((), ())), preferred_element_type=F32
    )


def contract_first(left, right):
    return lax.dot_general(
        left, right, (((0,), (0,)), ((), ())), preferred_element_type=F32
    )


def held(*arrays):
    count = len(arrays)

    def body(*refs):
        sources, targets, done = refs[:count], refs[count:-1], refs[-1]
        copies = [
            pltpu.make_async_copy(source, target, done.at[i])
            for i, (source, target) in enumerate(zip(sources, targets))
        ]
        for copy in copies:
            copy.start()
        for copy in copies:
            copy.wait()

    return pl.pallas_call(
        body,
        out_shape=[pltpu.VMEM(a.shape, a.dtype) for a in arrays],
        in_specs=[pl.BlockSpec(memory_space=pl.ANY)] * count,
        out_specs=[pl.BlockSpec(memory_space=pltpu.VMEM)] * count,
        scratch_shapes=[pltpu.SemaphoreType.DMA((count,))],
    )(*arrays)


def side_by_side(left, right, count):
    rows, width = left.shape

    def body(left_ref, right_ref, out_ref):
        pair = jnp.concatenate([left_ref[...], right_ref[...]], axis=1)
        out_ref[...] = jnp.broadcast_to(pair[None], (count, rows, 2 * width))

    return pl.pallas_call(
        body,
        out_shape=pltpu.VMEM((count, rows, 2 * width), left.dtype),
        in_specs=[pl.BlockSpec(memory_space=pltpu.VMEM)] * 2,
        out_specs=pl.BlockSpec(memory_space=pltpu.VMEM),
    )(left, right)


def swap_core(block):
    return lax.ppermute(block, "core", [(0, 1), (1, 0)])


def sum_over_x(block):
    ways = lax.axis_size("x")
    rows, columns = block.shape
    pieces = block.astype(BF16).reshape(ways, rows // ways, columns)
    return lax.all_to_all(pieces, "x", 0, 0).astype(F32).sum(0)


def swap_far(part, flips):
    pairs = [
        (2 * z + core, 2 * (z ^ flips[core]) + core)
        for z in range(4)
        for core in range(2)
    ]
    return lax.ppermute(part.astype(BF16), ("zh", "core"), pairs)


def deltas_of(part):
    units = part.shape[1] // 3
    gate_sum, up_sum, hidden_delta = (
        part[:, :units],
        part[:, units : 2 * units],
        part[:, 2 * units :],
    )
    gate_sigmoid = jax.nn.sigmoid(gate_sum)
    hidden = gate_sum * gate_sigmoid * up_sum
    gate_delta = (
        hidden_delta * up_sum * gate_sigmoid * (1.0 + gate_sum * (1.0 - gate_sigmoid))
    )
    up_delta = hidden_delta * gate_sum * gate_sigmoid
    return jnp.concatenate([hidden, gate_delta, up_delta], axis=1).astype(BF16)


def shards(tokens, gate_weight, up_weight, down_weight, out_grad):
    own, width = tokens.shape
    units = gate_weight.shape[1]
    sections = lax.axis_size(SECTION)
    rows = own * sections
    half = rows // 2
    gate_weight, up_weight, down_weight = held(gate_weight, up_weight, down_weight)
    both = side_by_side(tokens, out_grad, sections)
    both = lax.all_to_all(both, SECTION, 0, 0).reshape(rows, 2 * width)

    core = lax.axis_index("core")

    def part_of(which):
        side = lax.dynamic_slice_in_dim(both, which * half, half, 0)
        some_tokens, some_grads = side[:, :width], side[:, width:]
        return jnp.concatenate(
            [
                jnp.dot(some_tokens, gate_weight, preferred_element_type=F32),
                jnp.dot(some_tokens, up_weight, preferred_element_type=F32),
                contract_last(some_grads, down_weight),
            ],
            axis=1,
        )

    received = swap_core(part_of(1 - core).astype(BF16))
    part = sum_over_x(part_of(core) + received)

    piece = part.shape[0] // 2
    top, low = part[:piece], part[piece:]
    top_in, low_in = swap_far(top, (1, 3)), swap_far(low, (3, 1))
    top = top + top_in
    sent = top.astype(BF16)
    low_in, _ = lax.optimization_barrier((low_in, sent))
    top_in = swap_far(sent, (3, 1))
    low = low + low_in
    low_in = swap_far(low, (1, 3))
    mine = deltas_of(jnp.concatenate([top + top_in, low + low_in]))
    mine = lax.all_gather(mine, "x", axis=0, tiled=True)
    mine = mine.reshape(half, 3 * units)
    theirs = swap_core(mine)

    def ends_of(some):
        forward_part = jnp.dot(
            some[:, :units], down_weight, preferred_element_type=F32
        )
        backward_part = contract_last(
            some[:, units : 2 * units], gate_weight
        ) + contract_last(some[:, 2 * units :], up_weight)
        return jnp.concatenate([forward_part, backward_part], axis=1).astype(BF16)

    def in_order(own_rows, other_rows):
        first = core == 0
        return jnp.stack(
            [
                jnp.where(first, own_rows, other_rows),
                jnp.where(first, other_rows, own_rows),
            ]
        )

    ends = in_order(ends_of(mine), ends_of(theirs))
    whole = in_order(mine, theirs).reshape(rows, 3 * units)
    hidden, gate_delta, up_delta = (
        whole[:, :units],
        whole[:, units : 2 * units],
        whole[:, 2 * units :],
    )
    ends = ends.reshape(sections, own, 2 * width)
    ends = lax.all_to_all(ends, SECTION, 0, 0).astype(F32).sum(0).astype(BF16)
    all_tokens, all_grads = both[:, :width], both[:, width:]
    gate_grads = contract_first(all_tokens, gate_delta).astype(BF16)
    up_grads = contract_first(all_tokens, up_delta).astype(BF16)
    down_grads = contract_first(hidden, all_grads).astype(BF16)
    return (ends[:, :width], ends[:, width:], gate_grads, up_grads, down_grads)


def solution(mesh):
    fine = Mesh(
        mesh.devices.reshape(4, 8, 4, 4, 2), ("y", "zl", "zh", "x", "core")
    )
    return jax.shard_map(
        shards,
        mesh=fine,
        in_specs=(
            P(SECTION, FSDP),
            P(FSDP, SECTION),
            P(FSDP, SECTION),
            P(SECTION, FSDP),
            P(SECTION, FSDP),
        ),
        out_specs=(
            P(SECTION, FSDP),
            P(SECTION, FSDP),
            P(FSDP, SECTION),
            P(FSDP, SECTION),
            P(SECTION, FSDP),
        ),
        check_vma=False,
    )
```
